32 devices in a mesh: tm: 32 (over z, y, x, core).
Axes of the slice: x: 2, y: 2, z: 4, core: 2. Of those that a mesh axis runs over, the one named last changes fastest.
Arguments:
- transition: float32 [256, 256], replicated, may hold values from -1 to 1
- noise_var: float32 [256], replicated, may hold values from 0.001 to 0.1
- prior_mean: float32 [256], replicated, may hold values from -6 to 6
- prior_var: float32 [256], replicated, may hold values from 0.5 to 2
- obs_op: bfloat16 [32, 8, 128, 128], P('tm'), may hold values from -0.5 to 0.5
- obs_value: float32 [32, 8, 128], P('tm'), may hold values from -18 to 18
- obs_noise: float32 [32, 8, 128], P('tm'), may hold values from 10 to 100
- obs_block: int32 [32, 8], P('tm'), may hold values from 0 to 1
- obs_count: int32 [32], P('tm'), may hold values from 1 to 8, as said below
Outputs:
- smoothed_mean: float32 [32, 256], P('tm')
- smoothed_var: float32 [32, 256], P('tm')
The draws below stay inside these ranges and needn't reach their ends.
Inputs may be any that keep to these rules, and one draw needn't show every extreme that they name: Only the first obs_count[t] slots of step t carry observations; some step reports all 8.
All inputs are finite; a program needn't handle non-finite values.
Results may differ from the reference program's by a relative error of at most 0.024.
Values sent between devices are 32-bit elements; how exact they have to be, the bound alone decides.
A program may use at most 192 MiB of HBM per device.

```python
import math
import jax
import jax.numpy as jnp
from jax import lax

S = 256
BLOCK = 128
NB = 2
MAXB = 8
TIME = 32


def draw_transition(key, part):
    rate_key = jax.random.fold_in(key, 11)
    mix_key = jax.random.fold_in(key, 12)
    rates = jnp.exp(jax.random.uniform(rate_key, (S,), jnp.float32, math.log(0.5 / TIME), math.log(1.0 / 30.0)))
    mixing = jax.random.normal(mix_key, (S, S), jnp.float32) * (0.15 / math.sqrt(S))
    return jnp.diag(jnp.exp(-rates)) + (mixing - mixing.T)


def draw_obs_count(key, part):
    level = jax.random.randint(jax.random.fold_in(key, 21), (TIME,), 0, MAXB)
    position = jnp.arange(TIME, dtype=jnp.int32)
    rising = 1 + level * (position + 1) // TIME
    return jnp.where(position == TIME - 1, MAXB, rising).astype(jnp.int32)


def set_ends(result, stream_key, smallest, high):
    place = [jax.random.randint(jax.random.fold_in(stream_key, axis), (), 0, length) for axis, length in enumerate(result.shape)]
    widest = result.shape.index(max(result.shape))
    next_to = place[:widest] + [(place[widest] + 1) % result.shape[widest]] + place[widest + 1:]
    return result.at[tuple(place)].set(smallest).at[tuple(next_to)].set(high)


def level_of(stream_key, dims, pieces, least, largest):
    loudness = 1.0
    for axis_at, parts in pieces:
        steps = jax.random.uniform(jax.random.fold_in(jax.random.fold_in(stream_key, 6), axis_at), (parts,), jnp.float32, least / len(pieces), largest / len(pieces))
        loudness = loudness * jnp.repeat(jnp.exp(steps), dims[axis_at] // parts).reshape((-1,) + (1,) * (len(dims) - 1 - axis_at))
    return loudness


def normal_values(own_key, shape, scale, most, cuts=(), kind=jnp.bfloat16):
    loudness = level_of(own_key, shape, cuts, -0.22, 0.18) if cuts else 1.0
    result = jax.random.normal(own_key, shape, jnp.float32) * scale * loudness
    return jnp.minimum(jnp.maximum(result, -most), most).astype(kind)


def setup_inputs(seed: int = 0) -> dict:
    key_of = jax.random.split(jax.random.key(seed), 10)
    transition = draw_transition(jax.random.fold_in(key_of[9], 71), 0)
    noise_var = jnp.clip(jnp.exp(jax.random.uniform(key_of[1], (S,), jnp.float32, math.log(0.001), math.log(0.1))), 0.001, 0.1)
    prior_mean = normal_values(key_of[2], (S,), 1.0, 6.0, (), jnp.float32)
    prior_var = jnp.clip(jnp.exp(jax.random.uniform(key_of[3], (S,), jnp.float32, math.log(0.5), math.log(2.0))), 0.5, 2.0)
    obs_op = normal_values(key_of[4], (TIME, MAXB, BLOCK, BLOCK), BLOCK ** -0.5, 0.5, ((0, 32),))
    obs_value = normal_values(key_of[5], (TIME, MAXB, BLOCK), 3.0, 18.0, ((0, 32),), jnp.float32)
    obs_noise = jnp.clip(jnp.exp(math.log(100.0) - 2.3025851 * jax.random.uniform(key_of[6], (TIME, MAXB, BLOCK), jnp.float32) ** level_of(key_of[6], (TIME, MAXB, BLOCK), ((0, 32),), -0.2, 0.2)), 10.0, 100.0)
    obs_block = set_ends(jax.random.randint(key_of[7], (TIME, MAXB), 0, NB), jax.random.fold_in(key_of[7], 1), 0, NB - 1).astype(jnp.int32)
    obs_count = draw_obs_count(jax.random.fold_in(key_of[9], 71), 0)
    return {"transition": transition, "noise_var": noise_var, "prior_mean": prior_mean, "prior_var": prior_var, "obs_op": obs_op, "obs_value": obs_value, "obs_noise": obs_noise, "obs_block": obs_block, "obs_count": obs_count}


precise = lax.Precision.HIGHEST

def product(left, right):
    return jnp.dot(left.astype(jnp.float32), right.astype(jnp.float32), precision=precise, preferred_element_type=jnp.float32)

def step_information(obs_op, obs_value, obs_noise, obs_block, obs_count, nblocks):
    slots = obs_op.shape[0]
    width = obs_op.shape[2]
    active = (jnp.arange(slots, dtype=jnp.int32) < obs_count).astype(jnp.float32)
    chosen = (obs_block[:, None] == jnp.arange(nblocks, dtype=jnp.int32)[None, :]).astype(jnp.float32) * active[:, None]
    wide_op = obs_op.astype(jnp.float32)
    scaled = (wide_op / obs_noise[:, :, None]).astype(jnp.bfloat16)
    scaled = lax.optimization_barrier(scaled).astype(jnp.float32)
    slot_info = jnp.einsum('msi,msj->mij', scaled, wide_op, precision=precise)
    slot_shift = jnp.einsum('msi,ms->mi', wide_op, obs_value / obs_noise, precision=precise)
    block_info = jnp.einsum('ma,mij->aij', chosen, slot_info, precision=precise)
    block_shift = jnp.einsum('ma,mi->ai', chosen, slot_shift, precision=precise)
    dense = jnp.einsum('aij,ac->aicj', block_info, jnp.eye(nblocks, dtype=jnp.float32), precision=precise)
    return (dense.reshape(nblocks * width, nblocks * width), block_shift.reshape(nblocks * width))

def reference(transition, noise_var, prior_mean, prior_var, obs_op, obs_value, obs_noise, obs_block, obs_count):
    width = transition.shape[0]
    nblocks = width // BLOCK
    eye = jnp.eye(width, dtype=jnp.float32)
    process = jnp.diag(noise_var)

    def forward(carry, item):
        mean, cov, index = carry
        step_op, step_value, step_noise, step_block, step_count = item
        info, shift = step_information(step_op, step_value, step_noise, step_block, step_count, nblocks)
        first = index == 0
        pred_mean = jnp.where(first, prior_mean, product(transition, mean))
        pred_cov = jnp.where(first, jnp.diag(prior_var), product(product(transition, cov), transition.T) + process)
        factor = jnp.linalg.cholesky(pred_cov)
        pred_prec = jax.scipy.linalg.cho_solve((factor, True), eye)
        post_factor = jnp.linalg.cholesky(pred_prec + info)
        new_cov = jax.scipy.linalg.cho_solve((post_factor, True), eye)
        new_mean = product(new_cov, product(pred_prec, pred_mean) + shift)
        return ((new_mean, new_cov, index + 1), (new_mean, new_cov))
    start = (jnp.zeros((width,), jnp.float32), eye, jnp.zeros((), jnp.int32))
    _, (means, covs) = lax.scan(forward, start, (obs_op, obs_value, obs_noise, obs_block, obs_count))

    def backward(carry, item):
        next_mean, next_cov = carry
        mean, cov = item
        moved = product(transition, cov)
        predicted = product(moved, transition.T) + process
        factor = jnp.linalg.cholesky(predicted)
        gain = jax.scipy.linalg.cho_solve((factor, True), moved).T
        smooth_mean = mean + product(gain, next_mean - product(transition, mean))
        smooth_cov = cov + product(product(gain, next_cov - predicted), gain.T)
        return ((smooth_mean, smooth_cov), (smooth_mean, jnp.diagonal(smooth_cov)))
    _, (lower_mean, lower_var) = lax.scan(backward, (means[-1], covs[-1]), (means[:-1], covs[:-1]), reverse=True)
    smoothed_mean = jnp.concatenate([lower_mean, means[-1][None]], axis=0)
    smoothed_var = jnp.concatenate([lower_var, jnp.diagonal(covs[-1])[None]], axis=0)
    return (smoothed_mean, smoothed_var)
```

```python
import functools
import jax
import jax.numpy as jnp
from jax import lax
from jax.experimental import pallas as pl
from jax.experimental.pallas import tpu as pltpu
from jax.sharding import PartitionSpec as P

HALF = 128
TILE = 8
MESH = pl.DeviceIdType.MESH


def halves(value):
    high = value.astype(jnp.bfloat16)
    return high, (value - high.astype(jnp.float32)).astype(jnp.bfloat16)


def mm(left, right, dims=((1,), (0,))):
    left_high, left_low = halves(left)
    right_high, right_low = halves(right)
    return lax.dot_general(
        jnp.concatenate([left_low, left_high, left_high], axis=dims[0][0]),
        jnp.concatenate([right_high, right_low, right_high], axis=dims[1][0]),
        (dims, ((), ())),
        preferred_element_type=jnp.float32,
    )


NT = ((1,), (1,))
TN = ((0,), (0,))


def reciprocal(value):
    guess = pl.reciprocal(value, approx=True)
    guess = guess * (2.0 - value * guess)
    return guess * (2.0 - value * guess)


def invert_half(matrix):
    size = matrix.shape[0]
    lane = lax.broadcasted_iota(jnp.int32, (TILE, size), 1)
    row = lax.broadcasted_iota(jnp.int32, (TILE, size), 0)
    lane_all = lax.broadcasted_iota(jnp.int32, (1, size), 1)
    pivots = [
        jnp.broadcast_to(matrix[:TILE, j : j + 1], (TILE, size)) for j in range(TILE)
    ]
    for first in range(0, size, TILE):
        last = first + TILE
        more = range(last, min(last + TILE, size))
        wide = [
            jnp.broadcast_to(matrix[:, first + j : first + j + 1], (size, size))
            for j in range(TILE)
        ]
        beside = [jnp.broadcast_to(matrix[first:last, m : m + 1], (TILE, size)) for m in more]
        ahead = [
            jnp.broadcast_to(matrix[last : last + TILE, m : m + 1], (TILE, size)) for m in more
        ]
        inside = (lane >= first) & (lane < last)
        rows = jnp.where(inside, (lane - first == row).astype(jnp.float32), matrix[first:last])
        for j in range(0, TILE, 2):
            k = j + 1
            own = (row == j) | (row == k)
            a, b = (pivots[j][j : j + 1], pivots[k][j : j + 1])
            c, d = (pivots[j][k : k + 1], pivots[k][k : k + 1])
            scale = reciprocal(a * d - b * c)
            factor_j = jnp.where(own, jnp.where(row == j, -1.0, 0.0), pivots[j])
            factor_k = jnp.where(own, jnp.where(row == k, -1.0, 0.0), pivots[k])

            def swept(part):
                at_j, at_k = (part[j : j + 1], part[k : k + 1])
                new_j = (d * at_j - b * at_k) * scale
                new_k = (a * at_k - c * at_j) * scale
                return jnp.where(own, 0.0, part) - (factor_j * new_j + factor_k * new_k)

            pivots = pivots[: j + 2] + [swept(part) for part in pivots[j + 2 :]]
            beside = [swept(part) for part in beside]
            rows = swept(rows)

        def taken(start, columns, factors):
            pairs = [
                columns[j] * factors[j : j + 1] + columns[j + 1] * factors[j + 1 : j + 2]
                for j in range(0, TILE, 2)
            ]
            return start - ((pairs[0] + pairs[1]) + (pairs[2] + pairs[3]))

        pivots = [
            taken(old, [column[last : last + TILE] for column in wide], part)
            for old, part in zip(ahead, beside)
        ]
        kept = (lane_all < first) | (lane_all >= last)
        rest = taken(jnp.where(kept, matrix, 0.0), wide, rows)
        pieces = [rest[:first], rows, rest[last:]]
        matrix = jnp.concatenate([piece for piece in pieces if piece.shape[0]], axis=0)
    return matrix


def invert(matrix):
    size = matrix.shape[0]
    same = lax.broadcasted_iota(jnp.int32, (size, size), 0) == lax.broadcasted_iota(
        jnp.int32, (size, size), 1
    )
    diagonal = jnp.max(jnp.where(same, matrix, 0.0), axis=0, keepdims=True)
    unit = 1.0 / jnp.max(diagonal, axis=1, keepdims=True)
    matrix = matrix * unit
    side = matrix[:HALF, HALF:]
    top_first = invert_half(matrix[:HALF, :HALF])
    turned = mm(top_first, side)
    low_inverse = invert_half(matrix[HALF:, HALF:] - mm(side, turned, TN)) * unit
    across = mm(turned, low_inverse)
    top_inverse = top_first * unit + mm(across, turned, NT)
    return jnp.concatenate(
        [
            jnp.concatenate([top_inverse, -across], axis=1),
            jnp.concatenate([-across.T, low_inverse], axis=1),
        ],
        axis=0,
    )


def kernel(
    devices, rounds, transition, noise_var, prior_mean, prior_var, obs_op, obs_value, obs_noise,
    obs_block, obs_count, mean_out, var_out, cov, prec, lin, info, off, vec, step_lin,
    send_v, send_w, send_k, recv_v, recv_w, recv_k, sent, landed,
):
    size = transition.shape[0]
    slots, stations, width = obs_op.shape[1:]
    nblocks = size // width
    me = lax.axis_index("tm")

    barrier = pltpu.get_barrier_semaphore()
    for level in range(rounds):
        step = 1 << level

        @pl.when(me + step < devices)
        def _():
            pl.semaphore_signal(barrier, inc=1, device_id=(me + step,), device_id_type=MESH)

        @pl.when(me >= step)
        def _():
            pl.semaphore_signal(barrier, inc=1, device_id=(me - step,), device_id_type=MESH)

    noise = obs_noise[0]
    noise_cols = noise.T
    weighted = obs_value[0] / noise
    slot_row = lax.broadcasted_iota(jnp.int32, (TILE, stations), 0)
    scaled_slots, weight_slots, op_slots = ([], [], [])
    for m in range(slots):
        used = m < obs_count[0]
        block = obs_block[0, m]
        op = obs_op[0, m]
        scaled = (op.astype(jnp.float32) / noise_cols[:, m : m + 1]).astype(jnp.bfloat16)
        picks = [
            jnp.where(used & (block == a), 1.0, 0.0).astype(jnp.float32) for a in range(nblocks)
        ]
        wide = scaled.astype(jnp.float32)
        scaled_slots.append(
            jnp.concatenate([(wide * pick).astype(jnp.bfloat16) for pick in picks], axis=1)
        )
        row_weight = jnp.zeros((TILE, stations), jnp.float32)
        for a, pick in enumerate(picks):
            row_weight = row_weight + jnp.where(slot_row == a, weighted[m : m + 1] * pick, 0.0)
        weight_slots.append(row_weight)
        op_slots.append(op)
    ops = jnp.concatenate(op_slots, axis=0)
    stacked = lax.dot_general(
        jnp.concatenate(scaled_slots, axis=0),
        ops,
        (TN, ((), ())),
        preferred_element_type=jnp.float32,
    )
    shifts = mm(jnp.concatenate(weight_slots, axis=1), ops.astype(jnp.float32))
    blank = jnp.zeros((width, width), jnp.float32)
    info[...] = jnp.concatenate(
        [
            jnp.concatenate(
                [
                    stacked[a * width : (a + 1) * width] if a == c else blank
                    for c in range(nblocks)
                ],
                axis=1,
            )
            for a in range(nblocks)
        ],
        axis=0,
    )
    first_row = lax.broadcasted_iota(jnp.int32, (TILE, size), 0) == 0
    shift_row = jnp.concatenate([shifts[a : a + 1] for a in range(nblocks)], axis=1)
    vec[...] = jnp.where(first_row, shift_row, 0.0)

    start = me == 0
    same = lax.broadcasted_iota(jnp.int32, (size, size), 0) == lax.broadcasted_iota(
        jnp.int32, (size, size), 1
    )
    variance = jnp.where(start, prior_var[...], noise_var[...])
    cov[...] = jnp.where(same, variance, 0.0)
    prec[...] = jnp.where(same, 1.0 / variance, 0.0)
    moving = jnp.where(start, 0.0, 1.0).astype(jnp.float32)
    lin[...] = transition[...] * moving
    step_lin[...] = jnp.zeros_like(step_lin)
    off[...] = jnp.where(first_row, prior_mean[...] * (1.0 - moving), 0.0)

    peers = jnp.int32(0)
    for level in range(rounds):
        step = 1 << level
        peers = peers + jnp.where(me + step < devices, 1, 0) + jnp.where(me >= step, 1, 0)
    pl.semaphore_wait(barrier, peers)

    def copies(level, step):
        def one(source, target, kind, to):
            return pltpu.make_async_remote_copy(
                src_ref=source.at[level],
                dst_ref=target.at[level],
                send_sem=sent.at[level, kind],
                recv_sem=landed.at[level, kind],
                device_id=(to,),
                device_id_type=MESH,
            )

        return (
            one(send_v, recv_v, 0, me + step),
            one(send_w, recv_w, 1, me + step),
            one(send_k, recv_k, 2, me - step),
        )

    def turn(level, step):
        longer = (level > 0) & (me >= step // 2)
        link = jnp.where(longer, mm(lin[...], step_lin[...]), lin[...])
        lin[...] = link
        weighed = mm(prec[...], link)
        seen = mm(info[...], link)
        joint = invert(prec[...] + info[...])
        state = mm(vec[...] + mm(off[...], prec[...]), joint)
        copy_v, copy_w, copy_k = copies(level, step)
        right = me + step < devices
        left = me >= step

        @pl.when(level == rounds)
        def _():
            mean_out[...] = state[:1]
            var_out[...] = jnp.sum(jnp.where(same, joint, 0.0), axis=0, keepdims=True)

        @pl.when(level < rounds)
        def _():
            @pl.when(right)
            def _():
                send_v[level, :size] = joint
                send_v[level, size:] = state
                copy_v.start()

            passed = mm(joint, weighed)
            send_w[level] = passed
            send_k[level, :size] = mm(passed, seen, TN)
            send_k[level, size:] = mm(vec[...] - mm(off[...], info[...]), passed)

            @pl.when(left)
            def _():
                copy_v.wait_recv()
                copy_k.start()

            @pl.when(right)
            def _():
                copy_w.start()

            @pl.when(left)
            def _():
                spread = mm(lin[...], recv_v[level, :size])
                cov[...] = cov[...] + mm(spread, lin[...], NT)
                off[...] = off[...] + mm(recv_v[level, size:], lin[...], NT)

            prec[...] = invert(cov[...])

            @pl.when(left)
            def _():
                copy_w.wait_recv()
                step_lin[...] = recv_w[level]
                copy_k.wait_send()

            @pl.when(right)
            def _():
                copy_k.wait_recv()
                info[...] = info[...] + recv_k[level, :size]
                vec[...] = vec[...] + recv_k[level, size:]
                copy_v.wait_send()
                copy_w.wait_send()

        return step * 2

    lax.fori_loop(0, rounds + 1, turn, 1)


def local(
    transition, noise_var, prior_mean, prior_var, obs_op, obs_value, obs_noise, obs_block, obs_count
):
    devices = lax.axis_size("tm")
    size = transition.shape[0]
    rounds = (devices - 1).bit_length()
    slots = max(rounds, 1)
    vmem = pl.BlockSpec(memory_space=pltpu.VMEM)
    smem = pl.BlockSpec(memory_space=pltpu.SMEM)
    square = pltpu.VMEM((size, size), jnp.float32)
    rows = pltpu.VMEM((TILE, size), jnp.float32)
    tall = pltpu.VMEM((slots, size + TILE, size), jnp.float32)
    flat = pltpu.VMEM((slots, size, size), jnp.float32)
    row = jax.ShapeDtypeStruct((1, size), jnp.float32)
    return pl.pallas_call(
        functools.partial(kernel, devices, rounds),
        out_shape=(row, row),
        in_specs=[vmem] * 7 + [smem] * 2,
        out_specs=(vmem, vmem),
        scratch_shapes=[
            square, square, square, square, rows, rows,
            square,
            tall, flat, tall, tall, flat, tall,
            pltpu.SemaphoreType.DMA((slots, 3)),
            pltpu.SemaphoreType.DMA((slots, 3)),
        ],
        compiler_params=pltpu.CompilerParams(
            collective_id=0, has_side_effects=True, vmem_limit_bytes=40 * 1024 * 1024
        ),
    )(
        transition,
        noise_var[None],
        prior_mean[None],
        prior_var[None],
        obs_op,
        obs_value,
        obs_noise,
        obs_block,
        obs_count,
    )


def solution(mesh):
    return jax.shard_map(
        local,
        mesh=mesh,
        in_specs=(
            P(),
            P(),
            P(),
            P(),
            P("tm", None, None, None),
            P("tm", None, None),
            P("tm", None, None),
            P("tm", None),
            P("tm"),
        ),
        out_specs=(P("tm", None), P("tm", None)),
        check_vma=False,
    )
```
